768 devices in a mesh: row: 96 (over z_lo, x, y), col: 8 (over z_hi, core).
Axes of the slice: x: 4, y: 8, z: 12 (z_hi: 4, z_lo: 3; z = z_hi * 3 + z_lo), core: 2. Of those that a mesh axis runs over, the one named last changes fastest.
Arguments:
- amplitudes: bfloat16 [49152, 4096], P('row', 'col'), may hold values from -6 to 6
- integrals: bfloat16 [1536, 4096], P('row', 'col'), may hold values from -0.09375 to 0.09375
- residual_in: float32 [49152, 1536], P('row', 'col'), may hold values from -6 to 6
- amp_live: int32 [384, 4], P('row'), may hold values 0 or 1
- int_live: int32 [4, 96], replicated, may hold values 0 or 1
Outputs:
- residual_out: float32 [49152, 1536], P('row', 'col')
The draws below stay inside these ranges and needn't reach their ends.
All inputs are finite; a program needn't handle non-finite values. No bound on the sum of `amp_live` on one device may be relied on, other than what follows from the above.
Results may differ from the reference program's by a relative error of at most 0.0003.
Values may be sent and summed in bfloat16 or wider, within the bound.
No kernel may reach another device: no remote copies, remote signals or barrier semaphores. Data moves between devices by JAX's collectives and lax.ppermute only.
A program may use at most 32 MiB of HBM per device.

```python
import jax
import jax.numpy as jnp
from jax import lax

K = 4096
KTILE = 1024
RTILE = 128
VC_DEV = 16
KT = 4
ROWS = 49152
NV = 1536
N_ROW = 96


def plant(result, own_key, smallest, top_value):
    place = [jax.random.randint(jax.random.fold_in(own_key, axis), (), 0, length) for axis, length in enumerate(result.shape)]
    longest = result.shape.index(max(result.shape))
    beside = place[:longest] + [(place[longest] + 1) % result.shape[longest]] + place[longest + 1:]
    return result.at[tuple(place)].set(smallest).at[tuple(beside)].set(top_value)


def steps_of(rng, dims, pieces, low, high):
    loudness, own = 1.0, jax.random.fold_in(rng, 6)
    for position, blocks in pieces:
        heights = jnp.exp(jax.random.uniform(jax.random.fold_in(own, position), (blocks,), jnp.float32, low / len(pieces), high / len(pieces)))
        loudness = loudness * jnp.repeat(heights, dims[position] // blocks).reshape([-1 if axis == position else 1 for axis in range(len(dims))])
    return loudness


def centred(stream_key, shape, width, limit, cuts=(), kind=jnp.bfloat16):
    entries = width * jax.random.normal(stream_key, shape, jnp.float32)
    if cuts:
        entries = entries * steps_of(stream_key, shape, cuts, -0.22, 0.18)
    return jnp.clip(entries, -limit, limit).astype(kind)


def setup_inputs(seed: int = 0) -> dict:
    arg_keys = jax.random.split(jax.random.key(seed), 6)
    amplitudes = centred(arg_keys[0], (ROWS, K), 1.0, 6.0, ((0, 96), (1, 8)))
    integrals = centred(arg_keys[1], (NV, K), K ** -0.5, 0.09375, ((0, 96), (1, 8)))
    residual_in = centred(arg_keys[2], (ROWS, NV), 1.0, 6.0, ((0, 96), (1, 8)), jnp.float32)
    amp_live = plant((jax.random.randint(arg_keys[3], (ROWS // RTILE, KT), 0, 3) < 2).astype(jnp.int32), jax.random.fold_in(arg_keys[3], 1), 0, 1)
    int_live = plant((jax.random.randint(arg_keys[4], (KT, N_ROW), 0, 4) < 3).astype(jnp.int32), jax.random.fold_in(arg_keys[4], 1), 0, 1)
    return dict(amplitudes=amplitudes, integrals=integrals, residual_in=residual_in, amp_live=amp_live, int_live=int_live)


def reference(amplitudes, integrals, residual_in, amp_live, int_live):
    ktile_of = (jnp.arange(K) // KTILE).astype(jnp.int32)
    block_of = (jnp.arange(NV) // VC_DEV).astype(jnp.int32)
    keep_int = int_live[ktile_of][:, block_of]
    live_int = integrals * jnp.transpose(keep_int).astype(integrals.dtype)
    amp_blocks = amplitudes.reshape(ROWS // RTILE, RTILE, K)

    def one_tile(pair):
        block, keep = pair
        live_amp = block * keep[ktile_of][None, :].astype(block.dtype)
        return jnp.dot(live_amp, jnp.transpose(live_int), preferred_element_type=jnp.float32)

    ladder = lax.map(one_tile, (amp_blocks, amp_live)).reshape(ROWS, NV)
    return residual_in + ladder
```

```python
import numpy as np
import jax
import jax.numpy as jnp
from jax import lax
from jax.sharding import Mesh, PartitionSpec as P

AXES = ("zl", "x", "yh", "yl", "zh", "core")
SIZES = (3, 4, 4, 2, 4, 2)
ROW = ("zl", "x", "yh", "yl")
COL = ("zh", "core")
SCALE = 64.0


def blocks(q):
    return ((q, q), ((q + 1) % 4, q), ((q - 1) % 4, q), (q, (q + 2) % 4))


def deal():
    pairs = []
    for zl, x, yh, yl, q, j in np.ndindex(*SIZES):
        kt, n = blocks(q)[x]
        rp = 12 * (2 * n + j) + zl * 4 + yh
        source = rp * 8 + kt * 2 + yl
        target = int(np.ravel_multi_index((zl, x, yh, yl, q, j), SIZES))
        pairs.append((source, target))
    return pairs


def contract(left, right):
    return lax.dot_general(
        left, right, (((1,), (1,)), ((), ())), preferred_element_type=jnp.float32
    )


def shift(value, by):
    return lax.ppermute(value, "zh", [(i, (i + by) % 4) for i in range(4)])


def swap(value):
    return lax.ppermute(value, "core", [(0, 1), (1, 0)])


def gather(piece, axes, peers):
    copies = jnp.broadcast_to(piece[None], (peers,) + piece.shape)
    return lax.all_to_all(copies, axes, split_axis=0, concat_axis=0, tiled=True)


def shards(amplitudes, integrals, residual_in, amp_live, int_live):
    q, j = lax.axis_index("zh"), lax.axis_index("core")
    piece = lax.ppermute(integrals, AXES, deal())
    mine = amplitudes
    up, down = shift(amplitudes, -1), shift(amplitudes, 1)
    other = swap(mine)
    some = gather(piece, ("zl", "yh"), 12).reshape(192, 512)
    every = gather(some, ("x", "yl"), 8)
    up_other, down_other = swap(up), swap(down)

    def product(slot, own, sibling, kt, n):
        first = jnp.where(j == 0, every[2 * slot], every[2 * slot + 1])
        second = jnp.where(j == 0, every[2 * slot + 1], every[2 * slot])
        total = contract(first, own) + contract(second, sibling)
        rows = lax.dynamic_slice(int_live, (kt, 12 * (2 * n + j)), (1, 12))
        cols = lax.dynamic_slice(amp_live, (0, kt), (4, 1))
        keep_rows = jnp.repeat(rows.reshape(12), 16).astype(jnp.float32)
        keep_cols = jnp.repeat(cols.reshape(4), 128).astype(jnp.float32)
        return total * (keep_rows[:, None] * keep_cols[None, :])

    far = product(3, mine, other, q, (q + 2) % 4)
    arrived = shift((far * SCALE).astype(jnp.float16), 2)
    near = product(0, mine, other, q, q)
    near = near + product(1, up, up_other, (q + 1) % 4, q)
    near = near + product(2, down, down_other, (q + 3) % 4, q)
    total = near + arrived.astype(jnp.float32) * (1.0 / SCALE)
    return residual_in + jnp.transpose(total)


def solution(mesh):
    fine = Mesh(mesh.devices.reshape(SIZES), AXES)
    in_specs = (P(ROW, COL), P(ROW, COL), P(ROW, COL), P(ROW, None), P())
    return jax.shard_map(
        shards, mesh=fine, in_specs=in_specs, out_specs=P(ROW, COL), check_vma=False
    )
```

```python
import numpy as np
import jax
import jax.numpy as jnp
from jax import lax
from jax.sharding import Mesh, PartitionSpec as P

AXES = ("zl", "x", "yh", "yl", "zh", "core")
SIZES = (3, 4, 4, 2, 4, 2)
ROW = ("zl", "x", "yh", "yl")
COL = ("zh", "core")
SCALE = 64.0
CHUNKS = 1


def deal():
    pairs = []
    for zl, x, yh, yl, q, j in np.ndindex(*SIZES):
        source_row = 12 * (2 * x + j) + zl * 4 + yh
        source = source_row * 8 + q * 2 + (j ^ yl)
        target = int(np.ravel_multi_index((zl, x, yh, yl, q, j), SIZES))
        pairs.append((source, target))
    return pairs


def contract(left, right):
    return lax.dot_general(
        left, right, (((1,), (1,)), ((), ())), preferred_element_type=jnp.float32
    )


def swap(value):
    return lax.ppermute(value, "core", [(0, 1), (1, 0)])


def gather(piece, axes, peers):
    copies = jnp.broadcast_to(piece[None], (peers,) + piece.shape)
    return lax.all_to_all(copies, axes, split_axis=0, concat_axis=0, tiled=True)


def shards(amplitudes, integrals, residual_in, amp_live, int_live):
    q, j = lax.axis_index("zh"), lax.axis_index("core")
    piece = lax.ppermute(integrals, AXES, deal())
    other = swap(amplitudes)
    some = gather(piece, ("zl", "yh"), 12).reshape(192, 512)
    keep_int = lax.dynamic_slice(int_live, (q, 0), (1, 96)).reshape(4, 2, 12)
    keep_int = lax.dynamic_slice(keep_int, (0, j, 0), (4, 1, 12)).reshape(4, 12)
    keep_int = jnp.repeat(keep_int, 16, axis=1).astype(jnp.float32)
    keep_amp = lax.dynamic_slice(amp_live, (0, q), (4, 1)).reshape(4)
    keep_amp = jnp.repeat(keep_amp, 128).astype(jnp.float32)
    size = 192 // CHUNKS
    outs = []
    for part in range(CHUNKS):
        rows = slice(part * size, (part + 1) * size)
        every = gather(some[rows], ("yl", "x"), 8).reshape(2, 4 * size, 512)
        total = contract(every[0], amplitudes) + contract(every[1], other)
        total = total.reshape(4, size, 512)
        total = total * (keep_int[:, rows, None] * keep_amp[None, None, :])
        sent = (total * SCALE).astype(jnp.float16)
        came = lax.all_to_all(sent, "zh", split_axis=0, concat_axis=0, tiled=True)
        own = lax.dynamic_slice(total, (q, 0, 0), (1, size, 512))[0]
        for kt in range(4):
            term = came[kt].astype(jnp.float32) * (1.0 / SCALE)
            own = own + jnp.where(kt == q, 0.0, term)
        outs.append(own)
    total = jnp.concatenate(outs, axis=0)
    return residual_in + jnp.transpose(total)


def solution(mesh):
    fine = Mesh(mesh.devices.reshape(SIZES), AXES)
    in_specs = (P(ROW, COL), P(ROW, COL), P(ROW, COL), P(ROW, None), P())
    return jax.shard_map(
        shards, mesh=fine, in_specs=in_specs, out_specs=P(ROW, COL), check_vma=False
    )
```

```python
import numpy as np
import jax
import jax.numpy as jnp
from jax import lax
from jax.sharding import Mesh, PartitionSpec as P

AXES = ("zl", "x", "yh", "yl", "zh", "core")
SIZES = (3, 4, 4, 2, 4, 2)
ROW = ("zl", "x", "yh", "yl")
COL = ("zh", "core")
SCALE = 64.0
CHUNKS = 1


def deal():
    pairs = []
    for zl, x, yh, yl, q, j in np.ndindex(*SIZES):
        source_row = 12 * (2 * ((q + x) % 4) + j) + zl * 4 + yh
        source = source_row * 8 + q * 2 + (j ^ yl)
        target = int(np.ravel_multi_index((zl, x, yh, yl, q, j), SIZES))
        pairs.append((source, target))
    return pairs


def contract(left, right):
    return lax.dot_general(
        left, right, (((1,), (1,)), ((), ())), preferred_element_type=jnp.float32
    )


def swap(value):
    return lax.ppermute(value, "core", [(0, 1), (1, 0)])


def gather(piece, axes, peers):
    copies = jnp.broadcast_to(piece[None], (peers,) + piece.shape)
    return lax.all_to_all(copies, axes, split_axis=0, concat_axis=0, tiled=True)


def shards(amplitudes, integrals, residual_in, amp_live, int_live):
    q, j = lax.axis_index("zh"), lax.axis_index("core")
    piece = lax.ppermute(integrals, AXES, deal())
    other = swap(amplitudes)
    some = gather(piece, ("zl", "yh"), 12).reshape(192, 512)
    keep_int = lax.dynamic_slice(int_live, (q, 0), (1, 96)).reshape(4, 2, 12)
    keep_int = lax.dynamic_slice(keep_int, (0, j, 0), (4, 1, 12)).reshape(4, 12)
    keep_int = lax.dynamic_slice(jnp.concatenate([keep_int] * 2), (q, 0), (4, 12))
    keep_int = jnp.repeat(keep_int, 16, axis=1).astype(jnp.float32)
    keep_amp = lax.dynamic_slice(amp_live, (0, q), (4, 1)).reshape(4)
    keep_amp = jnp.repeat(keep_amp, 128).astype(jnp.float32)
    size = 192 // CHUNKS
    outs = []
    for part in range(CHUNKS):
        rows = slice(part * size, (part + 1) * size)
        every = gather(some[rows], ("yl", "x"), 8).reshape(2, 4 * size, 512)
        total = contract(every[0], amplitudes) + contract(every[1], other)
        total = total.reshape(4, size, 512)
        total = total * (keep_int[:, rows, None] * keep_amp[None, None, :])
        own = total[0]
        sent = (total * SCALE).astype(jnp.float16)
        for by in (2, 1, 3):
            pairs = [(i, (i + by) % 4) for i in range(4)]
            came = lax.ppermute(sent[by], "zh", pairs)
            own = own + came.astype(jnp.float32) * (1.0 / SCALE)
        outs.append(own)
    total = jnp.concatenate(outs, axis=0)
    return residual_in + jnp.transpose(total)


def solution(mesh):
    fine = Mesh(mesh.devices.reshape(SIZES), AXES)
    in_specs = (P(ROW, COL), P(ROW, COL), P(ROW, COL), P(ROW, None), P())
    return jax.shard_map(
        shards, mesh=fine, in_specs=in_specs, out_specs=P(ROW, COL), check_vma=False
    )
```

```python
import jax
import jax.numpy as jnp
from jax import lax
from jax.sharding import Mesh, PartitionSpec as P

AXES = ("zl", "x", "yh", "yl", "zh", "core")
SIZES = (3, 4, 4, 2, 4, 2)
ROW = ("zl", "x", "yh", "yl")
COL = ("zh", "core")
SCALE = 32.0


def contract(left, right):
    return lax.dot_general(
        left, right, (((1,), (1,)), ((), ())), preferred_element_type=jnp.float32
    )


def shift(value, by):
    pairs = []
    for i in range(4):
        pairs.append((2 * i, 2 * ((i + by) % 4)))
        pairs.append((2 * i + 1, 2 * ((i - by) % 4) + 1))
    return lax.ppermute(value, COL, pairs)


def swap(value):
    return lax.ppermute(value, "core", [(0, 1), (1, 0)])


def gather(piece, axes, peers):
    copies = jnp.broadcast_to(piece[None], (peers,) + piece.shape)
    return lax.all_to_all(copies, axes, split_axis=0, concat_axis=0, tiled=True)


def shards(amplitudes, integrals, residual_in, amp_live, int_live):
    q, j = lax.axis_index("zh"), lax.axis_index("core")
    some = gather(integrals, ("zl", "yh"), 12).reshape(192, 512)
    other = swap(amplitudes)
    some, other = lax.optimization_barrier((some, other))
    every = gather(some, ("yl", "x"), 8).reshape(2, 4, 3, 4, 16, 512)
    every = every.transpose(2, 1, 3, 0, 4, 5).reshape(4, 2, 192, 512)
    theirs = swap(lax.dynamic_slice(every, (0, 1 - j, 0, 0), (4, 1, 192, 512)))
    mine = lax.dynamic_slice(every, (0, j, 0, 0), (4, 1, 192, 512))
    total = contract(mine.reshape(768, 512), amplitudes)
    total = total + contract(theirs.reshape(768, 512), other)
    total = total.reshape(4, 192, 512)
    keep_amp = lax.dynamic_slice(amp_live, (0, q), (4, 1)).reshape(4)
    keep_amp = jnp.repeat(keep_amp, 128).astype(jnp.float32)[None, :]

    def product(slot):
        n = (q + slot) % 4
        keep_int = lax.dynamic_slice(int_live, (q, 12 * (2 * n + j)), (1, 12)).reshape(12)
        keep_int = jnp.repeat(keep_int, 16).astype(jnp.float32)[:, None]
        return lax.dynamic_slice(total, (n, 0, 0), (1, 192, 512))[0] * (keep_int * keep_amp)

    ahead = 1 + 2 * j
    relayed = shift((product(2) * SCALE).astype(jnp.float16), 1)
    behind = shift((product(4 - ahead) * SCALE).astype(jnp.float16), -1)
    both = product(ahead) * SCALE + relayed.astype(jnp.float32)
    both = shift(both.astype(jnp.float16), 1)
    came = behind.astype(jnp.float32) + both.astype(jnp.float32)
    return residual_in + jnp.transpose(product(0) + came * (1.0 / SCALE))


def solution(mesh):
    fine = Mesh(mesh.devices.reshape(SIZES), AXES)
    in_specs = (P(ROW, COL), P(ROW, COL), P(ROW, COL), P(ROW, None), P())
    return jax.shard_map(
        shards, mesh=fine, in_specs=in_specs, out_specs=P(ROW, COL), check_vma=False
    )
```

```python
import jax
import jax.numpy as jnp
from jax import lax
from jax.sharding import Mesh, PartitionSpec as P

AXES = ("zl", "x", "yh", "yl", "zh", "core")
SIZES = (3, 4, 4, 2, 4, 2)
ROW = ("zl", "x", "yh", "yl")
COL = ("zh", "core")
SCALE = 32.0


def contract(left, right):
    return lax.dot_general(
        left, right, (((1,), (1,)), ((), ())), preferred_element_type=jnp.float32
    )


def shift(value, by):
    pairs = []
    for i in range(4):
        pairs.append((2 * i, 2 * ((i + by) % 4)))
        pairs.append((2 * i + 1, 2 * ((i - by) % 4) + 1))
    return lax.ppermute(value, COL, pairs)


def swap(value):
    return lax.ppermute(value, "core", [(0, 1), (1, 0)])


def gather(piece, axes, peers):
    copies = jnp.broadcast_to(piece[None], (peers,) + piece.shape)
    return lax.all_to_all(copies, axes, split_axis=0, concat_axis=0, tiled=True)


def shards(amplitudes, integrals, residual_in, amp_live, int_live):
    q, j = lax.axis_index("zh"), lax.axis_index("core")
    some = gather(integrals, ("zl", "yh"), 12).reshape(192, 512)
    other = swap(amplitudes)
    every = gather(some, ("yl", "x"), 8).reshape(2, 4, 3, 4, 16, 512)
    ahead = 1 + 2 * j
    order = [(q + slot) % 4 for slot in (2, 4 - ahead, ahead, 0)]
    keep_amp = lax.dynamic_slice(amp_live, (0, q), (4, 1)).reshape(4)
    keep_amp = jnp.repeat(keep_amp, 128).astype(jnp.float32)[None, :]
    keep_int = []
    for n in order:
        keep = lax.dynamic_slice(int_live, (q, 12 * (2 * n + j)), (1, 12)).reshape(12)
        keep_int.append(jnp.repeat(keep, 16).astype(jnp.float32)[:, None])
    every, other, keep_int, keep_amp = lax.optimization_barrier((every, other, keep_int, keep_amp))
    every = every.transpose(2, 1, 3, 0, 4, 5).reshape(4, 2, 192, 512)
    theirs = swap(lax.dynamic_slice(every, (0, 1 - j, 0, 0), (4, 1, 192, 512)))
    mine = lax.dynamic_slice(every, (0, j, 0, 0), (4, 1, 192, 512))
    total = contract(mine.reshape(768, 512), amplitudes)
    total = total + contract(theirs.reshape(768, 512), other)
    total = total.reshape(4, 192, 512)
    products = []
    for n, keep in zip(order, keep_int):
        part = lax.dynamic_slice(total, (n, 0, 0), (1, 192, 512))[0]
        products.append(part * (keep * keep_amp))
    far, back, on, own = products
    relayed = shift((far * SCALE).astype(jnp.float16), 1)
    behind = shift((back * SCALE).astype(jnp.float16), -1)
    both = on * SCALE + relayed.astype(jnp.float32)
    both = shift(both.astype(jnp.float16), 1)
    came = behind.astype(jnp.float32) + both.astype(jnp.float32)
    return residual_in + jnp.transpose(own + came * (1.0 / SCALE))


def solution(mesh):
    fine = Mesh(mesh.devices.reshape(SIZES), AXES)
    in_specs = (P(ROW, COL), P(ROW, COL), P(ROW, COL), P(ROW, None), P())
    return jax.shard_map(
        shards, mesh=fine, in_specs=in_specs, out_specs=P(ROW, COL), check_vma=False
    )
```

```python
import jax
import jax.numpy as jnp
from jax import lax
from jax.sharding import Mesh, PartitionSpec as P

AXES = ("zl", "x", "yh", "yl", "zh", "core")
SIZES = (3, 4, 4, 2, 4, 2)
ROW = ("zl", "x", "yh", "yl")
COL = ("zh", "core")
LEAST = -100.0


def contract(left, right):
    return lax.dot_general(
        left, right, (((1,), (1,)), ((), ())), preferred_element_type=jnp.float32
    )


def shift(value, by):
    pairs = []
    for i in range(4):
        pairs.append((2 * i, 2 * ((i + by) % 4)))
        pairs.append((2 * i + 1, 2 * ((i - by) % 4) + 1))
    return lax.ppermute(value, COL, pairs)


def swap(value):
    return lax.ppermute(value, "core", [(0, 1), (1, 0)])


def pack(value, power):
    scaled = (value * jnp.exp2(14.0 - power)).astype(jnp.float16)
    return jnp.concatenate([scaled, jnp.broadcast_to(power, (16, 512)).astype(jnp.float16)])


def unpack(message):
    power = message[192:193].astype(jnp.float32)
    return message[:192].astype(jnp.float32) * jnp.exp2(power - 14.0), power


def gather(piece, axes, peers):
    copies = jnp.broadcast_to(piece[None], (peers,) + piece.shape)
    return lax.all_to_all(copies, axes, split_axis=0, concat_axis=0, tiled=True)


def shards(amplitudes, integrals, residual_in, amp_live, int_live):
    q, j = lax.axis_index("zh"), lax.axis_index("core")
    some = gather(integrals, ("zl", "yh"), 12).reshape(192, 512)
    other = swap(amplitudes)
    every = gather(some, ("yl", "x"), 8).reshape(2, 4, 3, 4, 16, 512)
    ahead = 1 + 2 * j
    order = [(q + slot) % 4 for slot in (2, 4 - ahead, ahead, 0)]
    keep_amp = lax.dynamic_slice(amp_live, (0, q), (4, 1)).reshape(4)
    keep_amp = jnp.repeat(keep_amp, 128).astype(jnp.float32)[None, :]
    keep_int = []
    for n in order:
        keep = lax.dynamic_slice(int_live, (q, 12 * (2 * n + j)), (1, 12)).reshape(12)
        keep_int.append(jnp.repeat(keep, 16).astype(jnp.float32)[:, None])
    every, other, keep_int, keep_amp = lax.optimization_barrier((every, other, keep_int, keep_amp))
    every = every.transpose(2, 1, 3, 0, 4, 5).reshape(4, 2, 192, 512)
    theirs = swap(lax.dynamic_slice(every, (0, 1 - j, 0, 0), (4, 1, 192, 512)))
    mine = lax.dynamic_slice(every, (0, j, 0, 0), (4, 1, 192, 512))
    total = contract(mine.reshape(768, 512), amplitudes)
    total = total + contract(theirs.reshape(768, 512), other)
    total = total.reshape(4, 192, 512)
    products = []
    for n, keep in zip(order, keep_int):
        part = lax.dynamic_slice(total, (n, 0, 0), (1, 192, 512))[0]
        products.append(part * (keep * keep_amp))
    far, back, on, own = products
    power = jnp.max(jnp.abs(total), axis=(0, 1))[None]
    power = jnp.ceil(jnp.log2(jnp.maximum(power, 2.0**LEAST))) + 1.0
    relayed = shift(pack(far, power), 1)
    behind = shift(pack(back, power), -1)
    value, other_power = unpack(relayed)
    both = shift(pack(on + value, jnp.maximum(power, other_power) + 1.0), 1)
    return residual_in + jnp.transpose(own + (unpack(behind)[0] + unpack(both)[0]))


def solution(mesh):
    fine = Mesh(mesh.devices.reshape(SIZES), AXES)
    in_specs = (P(ROW, COL), P(ROW, COL), P(ROW, COL), P(ROW, None), P())
    return jax.shard_map(
        shards, mesh=fine, in_specs=in_specs, out_specs=P(ROW, COL), check_vma=False
    )
```
